1024 devices in a mesh: dp: 16 (over x, y), expert: 64 (over z, core).
Axes of the slice: x: 4, y: 4, z: 32, core: 2. Of those that a mesh axis runs over, the one named last changes fastest.
Arguments:
- tokens: bfloat16 [131072, 2048], P(('dp', 'expert')), may hold values from -6 to 6
- routes: int32 [131072, 1], P(('dp', 'expert')), may hold values from 0 to 63; in each aligned block of 128 rows (0 to 127, 128 to 255, ...) at most 3 rows name the same one
- gates: float32 [131072, 1], P(('dp', 'expert')), may hold values from 0.2 to 1
- w_in: bfloat16 [64, 2048, 768], P('expert'), may hold values from -0.125 to 0.125
- w_out: bfloat16 [64, 768, 2048], P('expert'), may hold values from -0.21875 to 0.21875
- out_grad: bfloat16 [131072, 2048], P(('dp', 'expert')), may hold values from -3 to 3
Outputs:
- mixed: bfloat16 [131072, 2048], P(('dp', 'expert'))
- grad_tokens: bfloat16 [131072, 2048], P(('dp', 'expert'))
- grad_gates: float32 [131072, 1], P(('dp', 'expert'))
- grad_w_in: float32 [64, 2048, 768], P('expert', 'dp')
- grad_w_out: float32 [64, 768, 2048], P('expert', None, 'dp')
The draws below stay inside these ranges and needn't reach their ends.
Inputs may be any that keep to these rules, and one draw needn't show every extreme that they name: `routes`: each row names one expert. Among the rows of one device no expert is named more than 3 times, a bound that some block reaches.
All inputs are finite; a program needn't handle non-finite values.
Results may differ from the reference program's by a relative error of at most 0.015.
Values may be sent and summed in bfloat16 or wider, within the bound.
A program may use at most 64 MiB of HBM per device.

```python
import math
import jax
import jax.numpy as jnp
import numpy as np
from jax import lax

D = 2048
FW = 768
TOP = 1
TOK_DEV = 128
EXPERTS = 64
CAP = 3
TOKENS = 131072
N_DP = 16
N_EXPERT = 64


def level_of(own_key, extent, pieces, smallest, high):
    def one(axis_at, parts):
        draws = jax.random.uniform(jax.random.fold_in(jax.random.fold_in(own_key, 6), axis_at), (parts,), jnp.float32, smallest / len(pieces), high / len(pieces))
        return jnp.repeat(jnp.exp(draws), extent[axis_at] // parts).reshape((-1,) + (1,) * (len(extent) - axis_at - 1))

    factor_of = one(*pieces[0])
    for cut in pieces[1:]:
        factor_of = factor_of * one(*cut)
    return factor_of


def deal_out(own_key, own, number, rows, amount, top, limit, lean):
    sequence = jax.random.permutation(own_key, amount)
    crowded, usual = portions_of(amount, rows * top, limit, lean, True), portions_of(amount, rows * top, limit, lean, False)
    places = jnp.arange(amount)

    def named(sizes, turn):
        used = int((sizes > 0).sum())
        fixed = max(1, used // 4)
        moved = fixed + (places - fixed + turn * (used - fixed)) % max(1, amount - fixed)
        return jnp.zeros((amount,), jnp.int32).at[sequence[jnp.where(places < fixed, places, moved)]].set(jnp.asarray(sizes, jnp.int32))

    sizes = jnp.where(number % 4 == 0, named(crowded, number // 4), named(usual, number - number // 4 - 1))
    mixed = jax.random.permutation(jax.random.fold_in(own, 3), amount)
    giver, sink = mixed[0:amount // 2 * 2:2], mixed[1:amount // 2 * 2:2]
    room = jnp.minimum(sizes[giver] - 1, limit - sizes[sink]) // 2
    room = jnp.where((giver == sequence[0]) | (sink == sequence[0]) | (sizes[sink] == 0), 0, jnp.maximum(room, 0))
    moved = jax.random.randint(jax.random.fold_in(own, 4), (amount // 2,), 0, 1 << 20) % (room + 1)
    sizes = sizes.at[giver].add(-moved).at[sink].add(moved)
    members = jnp.searchsorted(jnp.cumsum(sizes), jnp.arange(rows * top), side="right").astype(jnp.int32)
    grid = members.reshape(top, rows).T
    grid = grid[jax.random.permutation(jax.random.fold_in(own, 1), rows)]
    turn = jax.random.randint(jax.random.fold_in(own, 2), (rows, 1), 0, top)
    return jnp.take_along_axis(grid, (jnp.arange(top)[None, :] + turn) % top, axis=1)


def portions_of(number_of, total, limit, slope, full):
    loads = [(1 << 20) // math.isqrt(grade ** slope) + 1 for grade in range(1, number_of + 1)]
    largest = limit if full else min(limit, max(-(-total // number_of), total * loads[0] // sum(loads)))
    least = 1 if total - largest >= number_of - 1 else 0
    holding, spare = [largest] + [least] * (number_of - 1), total - largest - least * (number_of - 1)
    while spare > 0:
        free = [i for i in range(1, number_of) if holding[i] < largest] or [i for i in range(1, number_of) if holding[i] < limit]
        pool, budget = sum([loads[i] for i in free]), spare
        for i in free:
            extra = min(limit - holding[i], max(1, budget * loads[i] // pool), spare)
            holding[i] = holding[i] + extra
            spare = spare - extra
    return np.array(holding)


def noise(key, shape, width, most, cuts=(), kind=jnp.bfloat16):
    result = width * jax.random.normal(key, shape, jnp.float32)
    if cuts:
        result = result * level_of(key, shape, cuts, -0.22, 0.18)
    return jnp.clip(result, -most, most).astype(kind)


def setup_inputs(seed: int = 0) -> dict:
    streams_of = jax.random.split(jax.random.key(seed), 7)
    tokens = noise(streams_of[0], (TOKENS, D), 1.0, 6.0, ((0, 1024),))
    routes_keys = jax.random.split(jax.random.fold_in(streams_of[1], 1), TOKENS // TOK_DEV)
    routes_turns = jax.random.permutation(jax.random.fold_in(streams_of[1], 3), TOKENS // TOK_DEV)
    routes = jax.vmap(lambda own, number: deal_out(jax.random.fold_in(streams_of[1], 2), own, number, TOK_DEV, EXPERTS, TOP, CAP, 2))(routes_keys, routes_turns).reshape((TOKENS, TOP))
    gates = jnp.clip(0.2 + 0.8 * jax.random.uniform(streams_of[2], (TOKENS, TOP), jnp.float32) ** level_of(streams_of[2], (TOKENS, TOP), ((0, 1024),), -0.2, 0.2), 0.2, 1.0)
    w_in = noise(streams_of[3], (EXPERTS, D, FW), D ** -0.5, 0.125, ((0, 64),))
    w_out = noise(streams_of[4], (EXPERTS, FW, D), FW ** -0.5, 0.21875, ((0, 64),))
    out_grad = noise(streams_of[5], (TOKENS, D), 0.5, 3.0, ((0, 1024),))
    return {"tokens": tokens, "routes": routes, "gates": gates, "w_in": w_in, "w_out": w_out, "out_grad": out_grad}


def rounded(value):
    return lax.optimization_barrier(value.astype(jnp.bfloat16)).astype(jnp.float32)


def reference(tokens, routes, gates, w_in, w_out, out_grad):
    pairs = TOK_DEV * TOP
    tok_four = tokens.reshape(N_DP, N_EXPERT, TOK_DEV, D)
    route_four = routes.reshape(N_DP, N_EXPERT, TOK_DEV, TOP)
    gate_four = gates.reshape(N_DP, N_EXPERT, TOK_DEV, TOP)
    grad_four = out_grad.reshape(N_DP, N_EXPERT, TOK_DEV, D)
    w_first = w_in.astype(jnp.float32)
    w_second = w_out.astype(jnp.float32)

    def group(carry, items):
        tok_group, route_group, gate_group, grad_group = items
        flat = route_group.reshape(N_EXPERT, pairs).astype(jnp.int32)
        onehot = (flat[:, :, None] == jnp.arange(EXPERTS, dtype=jnp.int32)[None, None, :]).astype(jnp.int32)
        earlier = (jnp.cumsum(onehot, axis=1) - onehot).astype(jnp.int32)
        slot = jnp.sum(onehot * earlier, axis=2).astype(jnp.int32)
        source = jnp.broadcast_to(jnp.arange(N_EXPERT, dtype=jnp.int32)[:, None], (N_EXPERT, pairs))
        repeated = jnp.repeat(tok_group, TOP, axis=1)
        scaled = (gate_group[:, :, :, None] * grad_group.astype(jnp.float32)[:, :, None, :]).astype(jnp.bfloat16)
        scaled = scaled.reshape(N_EXPERT, pairs, D)
        dispatched = jnp.zeros((EXPERTS, N_EXPERT, CAP, D), jnp.bfloat16).at[flat, source, slot].set(repeated)
        scaled_grad = jnp.zeros((EXPERTS, N_EXPERT, CAP, D), jnp.bfloat16).at[flat, source, slot].set(scaled)
        disp_wide = dispatched.astype(jnp.float32)
        grad_wide = scaled_grad.astype(jnp.float32)
        pre = jnp.einsum("escd,edf->escf", disp_wide, w_first)
        hidden = jax.nn.silu(pre).astype(jnp.bfloat16)
        hidden_wide = hidden.astype(jnp.float32)
        expert_out = jnp.einsum("escf,efd->escd", hidden_wide, w_second).astype(jnp.bfloat16)
        picked = expert_out[flat, source, slot].astype(jnp.float32).reshape(N_EXPERT, TOK_DEV, TOP, D)
        mixed = jnp.sum(gate_group[:, :, :, None] * picked, axis=2).astype(jnp.bfloat16)
        grad_gates = jnp.sum(picked * grad_group.astype(jnp.float32)[:, :, None, :], axis=3)
        sig = jax.nn.sigmoid(pre)
        grad_hidden = jnp.einsum("escd,efd->escf", grad_wide, w_second)
        grad_pre = (grad_hidden * sig * (1.0 + pre * (1.0 - sig))).astype(jnp.bfloat16)
        grad_pre_wide = grad_pre.astype(jnp.float32)
        grad_slots = jnp.einsum("escf,edf->escd", grad_pre_wide, w_first).astype(jnp.bfloat16)
        back = grad_slots[flat, source, slot].astype(jnp.float32).reshape(N_EXPERT, TOK_DEV, TOP, D)
        grad_tok = jnp.sum(back, axis=2).astype(jnp.bfloat16)
        part_in = jnp.einsum("escd,escf->edf", disp_wide, grad_pre_wide)
        part_out = jnp.einsum("escf,escd->efd", hidden_wide, grad_wide)
        carry = (carry[0] + rounded(part_in), carry[1] + rounded(part_out))
        return carry, (mixed, grad_tok, grad_gates)

    start = (jnp.zeros((EXPERTS, D, FW), jnp.float32), jnp.zeros((EXPERTS, FW, D), jnp.float32))
    totals, stacked = lax.scan(group, start, (tok_four, route_four, gate_four, grad_four))
    mixed = stacked[0].reshape(TOKENS, D)
    grad_tokens = stacked[1].reshape(TOKENS, D)
    grad_gates = stacked[2].reshape(TOKENS, TOP)
    return mixed, grad_tokens, grad_gates, totals[0], totals[1]
```

```python
import functools

import jax
import jax.numpy as jnp
from jax import lax
from jax.experimental import pallas as pl
from jax.experimental.pallas import tpu as pltpu
from jax.sharding import PartitionSpec as P

MESH = pl.DeviceIdType.MESH
LANES = 128
F32 = jnp.float32
BF16 = jnp.bfloat16


def dot(left, right, dims):
    return lax.dot_general(left, right, ((dims[0], dims[1]), ((), ())), preferred_element_type=F32)


def kernel(
    groups,
    experts,
    capacity,
    tok_hbm,
    grad_hbm,
    w_in_hbm,
    w_out_hbm,
    routes_ref,
    gates_ref,
    mixed_ref,
    grad_tok_ref,
    grad_gates_ref,
    first_ref,
    second_ref,
    tok,
    cot,
    w_in,
    w_out,
    select,
    stage,
    x_send,
    x_recv,
    g_send,
    g_recv,
    o_send,
    o_recv,
    b_send,
    b_recv,
    xs,
    gs,
    pre,
    hidden,
    grad_pre,
    first_send,
    first_recv,
    second_send,
    second_recv,
    load_sem,
    own_sem,
    send_sem,
    recv_sem,
):
    dp = lax.axis_index("dp")
    me = lax.axis_index("expert")
    z, core = me // 2, me % 2
    ring = experts // 2
    rows, width = tok.shape
    slots = experts * capacity
    chunks = width // LANES
    block = capacity * chunks
    hid = hidden.shape[1]

    loads = [
        pltpu.make_async_copy(source, target, load_sem.at[i])
        for i, (source, target) in enumerate(
            ((tok_hbm, tok), (grad_hbm, cot), (w_in_hbm, w_in), (w_out_hbm, w_out))
        )
    ]
    for load in loads:
        load.start()

    barrier = pltpu.get_barrier_semaphore()

    def greet_expert(k, _):
        pl.semaphore_signal(
            barrier, inc=1, device_id=(dp, (me + k) % experts), device_id_type=MESH
        )
        return 0

    def greet_group(k, _):
        pl.semaphore_signal(
            barrier, inc=1, device_id=((dp + k) % groups, me), device_id_type=MESH
        )
        return 0

    lax.fori_loop(1, experts, greet_expert, 0)
    lax.fori_loop(1, groups, greet_group, 0)

    def scatter(source, target, which):
        pltpu.make_async_copy(source.at[me], target.at[me], own_sem.at[which]).start()

        def send(place):
            pltpu.make_async_remote_copy(
                src_ref=source.at[place],
                dst_ref=target.at[me],
                send_sem=send_sem.at[which],
                recv_sem=recv_sem.at[which],
                device_id=(dp, place),
                device_id_type=MESH,
            ).start()

        def step(i, _):
            far = ring // 2 - (i + 1) // 2
            sign = 1 - 2 * (i % 2)
            there = (z + sign * far + ring) % ring
            send(there * 2 + core)
            send(there * 2 + 1 - core)
            return 0

        lax.fori_loop(0, ring - 1, step, 0)
        send(z * 2 + 1 - core)

    def arrived(target, which):
        others = target.at[pl.ds(0, target.shape[0] - 1)]
        pltpu.make_async_copy(target.at[0], target.at[0], own_sem.at[which]).wait()
        pltpu.make_async_copy(others, others, recv_sem.at[which]).wait()

    def sent(target, which):
        others = target.at[pl.ds(0, target.shape[0] - 1)]
        pltpu.make_async_copy(others, others, send_sem.at[which]).wait()

    def spread(j, value):
        stage[pl.ds(j, slots, stride=chunks), :] = value

    def gathered(j):
        return stage[pl.ds(j, slots, stride=chunks), :]

    def lanes(j):
        return pl.ds(pl.multiple_of(j * LANES, LANES), LANES)

    def to_blocks(target):
        def step(e, _):
            part = stage[pl.ds(pl.multiple_of(e * block, block), block), :]
            target[e] = part.astype(BF16)
            return 0

        lax.fori_loop(0, experts, step, 0, unroll=4)

    def from_blocks(source):
        def step(e, _):
            stage[pl.ds(pl.multiple_of(e * block, block), block), :] = source[e].astype(F32)
            return 0

        lax.fori_loop(0, experts, step, 0, unroll=4)

    def to_rows(source, target):
        from_blocks(source)

        def step(j, _):
            target[:, lanes(j)] = gathered(j).astype(BF16)
            return 0

        lax.fori_loop(0, chunks, step, 0)

    route = routes_ref[...]
    onehot = (route == lax.broadcasted_iota(jnp.int32, (rows, experts), 1)).astype(F32)
    before = (
        lax.broadcasted_iota(jnp.int32, (rows, rows), 0)
        > lax.broadcasted_iota(jnp.int32, (rows, rows), 1)
    ).astype(BF16)
    earlier = dot(before, onehot.astype(BF16), ((1,), (0,)))
    slot = jnp.sum(onehot * earlier, axis=1, keepdims=True).astype(jnp.int32)
    place = route * capacity + slot
    select[...] = (place == lax.broadcasted_iota(jnp.int32, (rows, slots), 1)).astype(BF16)

    loads[0].wait()

    def pick_tokens(j, _):
        spread(j, dot(select[...], tok[:, lanes(j)], ((0,), (0,))))
        return 0

    lax.fori_loop(0, chunks, pick_tokens, 0)
    to_blocks(x_send)
    pl.semaphore_wait(barrier, experts - 1 + groups - 1)
    scatter(x_send, x_recv, 0)

    loads[1].wait()

    def pick_grads(j, _):
        scaled = (gates_ref[...] * cot[:, lanes(j)].astype(F32)).astype(BF16)
        spread(j, dot(select[...], scaled, ((0,), (0,))))
        return 0

    lax.fori_loop(0, chunks, pick_grads, 0)
    to_blocks(g_send)
    scatter(g_send, g_recv, 1)

    loads[2].wait()
    loads[3].wait()
    arrived(x_recv, 0)
    to_rows(x_recv, xs)

    def wide(j):
        return pl.ds(pl.multiple_of(j * 256, 256), 256)

    def forward(j, _):
        value = dot(xs[...], w_in[:, wide(j)], ((1,), (0,)))
        pre[:, wide(j)] = value
        hidden[:, wide(j)] = (value / (1.0 + jnp.exp(-value))).astype(BF16)
        return 0

    lax.fori_loop(0, hid // 256, forward, 0)

    def project(j, _):
        value = dot(hidden[...], w_out[:, wide(j)], ((1,), (0,)))
        spread(2 * j, value[:, :LANES])
        spread(2 * j + 1, value[:, LANES:])
        return 0

    lax.fori_loop(0, width // 256, project, 0)
    to_blocks(o_send)
    scatter(o_send, o_recv, 2)

    arrived(g_recv, 1)
    to_rows(g_recv, gs)

    def backward(j, _):
        value = dot(gs[...], w_out[wide(j), :], ((1,), (1,)))
        at = pre[:, wide(j)]
        sig = 1.0 / (1.0 + jnp.exp(-at))
        grad_pre[:, wide(j)] = (value * sig * (1.0 + at * (1.0 - sig))).astype(BF16)
        return 0

    lax.fori_loop(0, hid // 256, backward, 0)

    def unproject(j, _):
        value = dot(grad_pre[...], w_in[wide(j), :], ((1,), (1,)))
        spread(2 * j, value[:, :LANES])
        spread(2 * j + 1, value[:, LANES:])
        return 0

    lax.fori_loop(0, width // 256, unproject, 0)
    to_blocks(b_send)
    scatter(b_send, b_recv, 3)

    def weight_terms(k, _):
        to = (dp + k) % groups
        first_send[to] = dot(xs[:, lanes(to)], grad_pre[...], ((0,), (0,))).astype(BF16)
        second_send[to] = dot(hidden[...], gs[:, lanes(to)], ((0,), (0,))).astype(BF16)
        return to

    def share(k, _):
        to = weight_terms(k, 0)
        for which, source, target in ((4, first_send, first_recv), (5, second_send, second_recv)):
            pltpu.make_async_remote_copy(
                src_ref=source.at[to],
                dst_ref=target.at[dp],
                send_sem=send_sem.at[which],
                recv_sem=recv_sem.at[which],
                device_id=(to, me),
                device_id_type=MESH,
            ).start()
        return 0

    lax.fori_loop(1, groups, share, 0)
    weight_terms(0, 0)
    for which, source, target in ((4, first_send, first_recv), (5, second_send, second_recv)):
        pltpu.make_async_copy(source.at[dp], target.at[dp], own_sem.at[which]).start()

    arrived(o_recv, 2)
    from_blocks(o_recv)
    grad_gates_ref[...] = jnp.zeros_like(grad_gates_ref)

    def mix(j, _):
        picked = dot(select[...], gathered(j).astype(BF16), ((1,), (0,)))
        mixed_ref[:, lanes(j)] = (gates_ref[...] * picked).astype(BF16)
        grad_gates_ref[...] += jnp.sum(
            picked * cot[:, lanes(j)].astype(F32), axis=1, keepdims=True
        )
        return 0

    lax.fori_loop(0, chunks, mix, 0)

    arrived(first_recv, 4)
    arrived(second_recv, 5)

    def add_terms(target, source):
        def step(r, _):
            part = pl.ds(pl.multiple_of(r * 16, 16), 16)
            total = source[0, part, :].astype(F32)
            for i in range(1, groups):
                total = total + source[i, part, :].astype(F32)
            target[part, :] = total
            return 0

        lax.fori_loop(0, target.shape[0] // 16, step, 0)

    add_terms(first_ref, first_recv)
    add_terms(second_ref, second_recv)

    arrived(b_recv, 3)
    from_blocks(b_recv)

    def unmix(j, _):
        picked = dot(select[...], gathered(j).astype(BF16), ((1,), (0,)))
        grad_tok_ref[:, lanes(j)] = picked.astype(BF16)
        return 0

    lax.fori_loop(0, chunks, unmix, 0)
    sent(x_send, 0)
    sent(g_send, 1)
    sent(o_send, 2)
    sent(b_send, 3)
    sent(first_send, 4)
    sent(second_send, 5)


def local(tokens, routes, gates, w_in, w_out, out_grad):
    groups, experts = lax.axis_size("dp"), lax.axis_size("expert")
    rows, width = tokens.shape
    capacity = max(2, 3 * rows * routes.shape[1] // (2 * experts))
    slots = experts * capacity
    hid = w_in.shape[2]
    chunks = width // LANES
    blocks = pltpu.VMEM((experts, capacity * chunks, LANES), BF16)
    first = pltpu.VMEM((groups, width // groups, hid), BF16)
    second = pltpu.VMEM((groups, hid, width // groups), BF16)
    vmem = pl.BlockSpec(memory_space=pltpu.VMEM)
    hbm = pl.BlockSpec(memory_space=pl.ANY)
    mixed, grad_tokens, grad_gates, grad_first, grad_second = pl.pallas_call(
        functools.partial(kernel, groups, experts, capacity),
        out_shape=(
            jax.ShapeDtypeStruct((rows, width), BF16),
            jax.ShapeDtypeStruct((rows, width), BF16),
            jax.ShapeDtypeStruct((rows, 1), F32),
            jax.ShapeDtypeStruct((width // groups, hid), F32),
            jax.ShapeDtypeStruct((hid, width // groups), F32),
        ),
        in_specs=[hbm, hbm, hbm, hbm, vmem, vmem],
        out_specs=[vmem] * 5,
        scratch_shapes=[
            pltpu.VMEM((rows, width), BF16),
            pltpu.VMEM((rows, width), BF16),
            pltpu.VMEM((width, hid), BF16),
            pltpu.VMEM((hid, width), BF16),
            pltpu.VMEM((rows, slots), BF16),
            pltpu.VMEM((slots * chunks, LANES), F32),
            *([blocks] * 8),
            pltpu.VMEM((slots, width), BF16),
            pltpu.VMEM((slots, width), BF16),
            pltpu.VMEM((slots, hid), F32),
            pltpu.VMEM((slots, hid), BF16),
            pltpu.VMEM((slots, hid), BF16),
            first,
            first,
            second,
            second,
            pltpu.SemaphoreType.DMA((4,)),
            pltpu.SemaphoreType.DMA((6,)),
            pltpu.SemaphoreType.DMA((6,)),
            pltpu.SemaphoreType.DMA((6,)),
        ],
        compiler_params=pltpu.CompilerParams(
            collective_id=0, has_side_effects=True, vmem_limit_bytes=50 * 2**20
        ),
        cost_estimate=pl.CostEstimate(
            flops=12 * slots * width * hid,
            bytes_accessed=12 * width * hid,
            transcendentals=2 * slots * hid,
        ),
    )(tokens, out_grad, w_in[0], w_out[0], routes, gates)
    return (mixed, grad_tokens, grad_gates, grad_first[None], grad_second[None])


def solution(mesh):
    placed = (
        P(("dp", "expert"), None),
        P(("dp", "expert"), None),
        P(("dp", "expert"), None),
        P("expert", None, None),
        P("expert", None, None),
        P(("dp", "expert"), None),
    )
    return jax.shard_map(
        local,
        mesh=mesh,
        in_specs=placed,
        out_specs=(
            P(("dp", "expert"), None),
            P(("dp", "expert"), None),
            P(("dp", "expert"), None),
            P("expert", "dp", None),
            P("expert", None, "dp"),
        ),
        check_vma=False,
    )
```

```python
import functools
import math

import jax
import jax.numpy as jnp
from jax import lax
from jax.experimental import pallas as pl
from jax.experimental.pallas import tpu as pltpu
from jax.sharding import PartitionSpec as P

MESH = pl.DeviceIdType.MESH
LANES = 128
F32 = jnp.float32
BF16 = jnp.bfloat16


def dot(left, right, dims):
    return lax.dot_general(left, right, ((dims[0], dims[1]), ((), ())), preferred_element_type=F32)


def kernel(
    groups,
    experts,
    capacity,
    tok_hbm,
    grad_hbm,
    w_in_hbm,
    w_out_hbm,
    routes_ref,
    gates_ref,
    mixed_ref,
    grad_tok_ref,
    grad_gates_ref,
    first_ref,
    second_ref,
    tok,
    cot,
    w_in,
    w_out,
    select,
    stage,
    x_send,
    x_recv,
    g_send,
    g_recv,
    o_send,
    o_recv,
    b_send,
    b_recv,
    xs,
    gs,
    pre,
    hidden,
    grad_pre,
    first_send,
    first_recv,
    second_send,
    second_recv,
    load_sem,
    own_sem,
    send_sem,
    recv_sem,
):
    dp = lax.axis_index("dp")
    me = lax.axis_index("expert")
    z, core = me // 2, me % 2
    ring = experts // 2
    rows, width = tok.shape
    slots = experts * capacity
    chunks = width // LANES
    block = capacity * chunks
    hid = hidden.shape[1]

    loads = [
        pltpu.make_async_copy(source, target, load_sem.at[i])
        for i, (source, target) in enumerate(
            ((tok_hbm, tok), (grad_hbm, cot), (w_in_hbm, w_in), (w_out_hbm, w_out))
        )
    ]
    for load in loads:
        load.start()

    barrier = pltpu.get_barrier_semaphore()

    def greet_expert(k, _):
        pl.semaphore_signal(
            barrier, inc=1, device_id=(dp, (me + k) % experts), device_id_type=MESH
        )
        return 0

    def greet_group(k, _):
        pl.semaphore_signal(
            barrier, inc=1, device_id=((dp + k) % groups, me), device_id_type=MESH
        )
        return 0

    lax.fori_loop(1, experts, greet_expert, 0)
    lax.fori_loop(1, groups, greet_group, 0)

    def scatter(source, target, which):
        pltpu.make_async_copy(source.at[me], target.at[me], own_sem.at[which]).start()

        def send(place):
            pltpu.make_async_remote_copy(
                src_ref=source.at[place],
                dst_ref=target.at[me],
                send_sem=send_sem.at[which],
                recv_sem=recv_sem.at[which],
                device_id=(dp, place),
                device_id_type=MESH,
            ).start()

        def step(i, _):
            far = ring // 2 - (i + 1) // 2
            sign = 1 - 2 * (i % 2)
            there = (z + sign * far + ring) % ring
            send(there * 2 + core)
            send(there * 2 + 1 - core)
            return 0

        lax.fori_loop(0, ring - 1, step, 0)
        send(z * 2 + 1 - core)

    def arrived(target, which):
        others = target.at[pl.ds(0, target.shape[0] - 1)]
        pltpu.make_async_copy(target.at[0], target.at[0], own_sem.at[which]).wait()
        pltpu.make_async_copy(others, others, recv_sem.at[which]).wait()

    def sent(target, which):
        others = target.at[pl.ds(0, target.shape[0] - 1)]
        pltpu.make_async_copy(others, others, send_sem.at[which]).wait()

    def spread(j, value):
        stage[pl.ds(j, slots, stride=chunks), :] = value

    def gathered(j):
        return stage[pl.ds(j, slots, stride=chunks), :]

    def lanes(j):
        return pl.ds(pl.multiple_of(j * LANES, LANES), LANES)

    def to_blocks(target):
        def step(e, _):
            part = stage[pl.ds(pl.multiple_of(e * block, block), block), :]
            target[e] = part.astype(BF16)
            return 0

        lax.fori_loop(0, experts, step, 0, unroll=4)

    def from_blocks(source):
        def step(e, _):
            stage[pl.ds(pl.multiple_of(e * block, block), block), :] = source[e].astype(F32)
            return 0

        lax.fori_loop(0, experts, step, 0, unroll=4)

    def to_rows(source, target):
        from_blocks(source)

        def step(j, _):
            target[:, lanes(j)] = gathered(j).astype(BF16)
            return 0

        lax.fori_loop(0, chunks, step, 0)

    route = routes_ref[...]
    onehot = (route == lax.broadcasted_iota(jnp.int32, (rows, experts), 1)).astype(F32)
    before = (
        lax.broadcasted_iota(jnp.int32, (rows, rows), 0)
        > lax.broadcasted_iota(jnp.int32, (rows, rows), 1)
    ).astype(BF16)
    earlier = dot(before, onehot.astype(BF16), ((1,), (0,)))
    slot = jnp.sum(onehot * earlier, axis=1, keepdims=True).astype(jnp.int32)
    place = route * capacity + slot
    select[...] = (place == lax.broadcasted_iota(jnp.int32, (rows, slots), 1)).astype(BF16)

    loads[0].wait()

    def pick_tokens(j, _):
        spread(j, dot(select[...], tok[:, lanes(j)], ((0,), (0,))))
        return 0

    lax.fori_loop(0, chunks, pick_tokens, 0)
    to_blocks(x_send)
    pl.semaphore_wait(barrier, experts - 1 + groups - 1)
    scatter(x_send, x_recv, 0)

    loads[1].wait()

    def pick_grads(j, _):
        scaled = (gates_ref[...] * cot[:, lanes(j)].astype(F32)).astype(BF16)
        spread(j, dot(select[...], scaled, ((0,), (0,))))
        return 0

    lax.fori_loop(0, chunks, pick_grads, 0)
    to_blocks(g_send)
    scatter(g_send, g_recv, 1)

    loads[2].wait()
    loads[3].wait()
    arrived(x_recv, 0)
    to_rows(x_recv, xs)

    def wide(j):
        return pl.ds(pl.multiple_of(j * 256, 256), 256)

    def forward(j, _):
        value = dot(xs[...], w_in[:, wide(j)], ((1,), (0,)))
        pre[:, wide(j)] = value
        hidden[:, wide(j)] = (value / (1.0 + jnp.exp(-value))).astype(BF16)
        return 0

    lax.fori_loop(0, hid // 256, forward, 0)

    def project(j, _):
        value = dot(hidden[...], w_out[:, wide(j)], ((1,), (0,)))
        spread(2 * j, value[:, :LANES])
        spread(2 * j + 1, value[:, LANES:])
        return 0

    lax.fori_loop(0, width // 256, project, 0)
    to_blocks(o_send)
    sent(g_send, 1)
    scatter(o_send, o_recv, 2)

    arrived(g_recv, 1)
    to_rows(g_recv, gs)

    def backward(j, _):
        value = dot(gs[...], w_out[wide(j), :], ((1,), (1,)))
        at = pre[:, wide(j)]
        sig = 1.0 / (1.0 + jnp.exp(-at))
        grad_pre[:, wide(j)] = (value * sig * (1.0 + at * (1.0 - sig))).astype(BF16)
        return 0

    lax.fori_loop(0, hid // 256, backward, 0)

    side = math.isqrt(groups)

    def weight_terms(k, _):
        turn = k * 5 % groups
        to = (dp // side + turn // side) % side * side + (dp + turn) % side
        first_send[to] = dot(xs[:, lanes(to)], grad_pre[...], ((0,), (0,))).astype(BF16)
        second_send[to] = dot(hidden[...], gs[:, lanes(to)], ((0,), (0,))).astype(BF16)
        return to

    def share(k, _):
        to = weight_terms(k, 0)
        for which, source, target in ((4, first_send, first_recv), (5, second_send, second_recv)):
            pltpu.make_async_remote_copy(
                src_ref=source.at[to],
                dst_ref=target.at[dp],
                send_sem=send_sem.at[which],
                recv_sem=recv_sem.at[which],
                device_id=(to, me),
                device_id_type=MESH,
            ).start()
        return 0

    lax.fori_loop(1, groups, share, 0)
    weight_terms(0, 0)
    for which, source, target in ((4, first_send, first_recv), (5, second_send, second_recv)):
        pltpu.make_async_copy(source.at[dp], target.at[dp], own_sem.at[which]).start()

    def unproject(j, _):
        value = dot(grad_pre[...], w_in[wide(j), :], ((1,), (1,)))
        spread(2 * j, value[:, :LANES])
        spread(2 * j + 1, value[:, LANES:])
        return 0

    lax.fori_loop(0, width // 256, unproject, 0)
    to_blocks(b_send)
    scatter(b_send, b_recv, 3)

    arrived(o_recv, 2)
    from_blocks(o_recv)
    grad_gates_ref[...] = jnp.zeros_like(grad_gates_ref)

    def mix(j, _):
        picked = dot(select[...], gathered(j).astype(BF16), ((1,), (0,)))
        mixed_ref[:, lanes(j)] = (gates_ref[...] * picked).astype(BF16)
        grad_gates_ref[...] += jnp.sum(
            picked * cot[:, lanes(j)].astype(F32), axis=1, keepdims=True
        )
        return 0

    lax.fori_loop(0, chunks, mix, 0)

    arrived(first_recv, 4)
    arrived(second_recv, 5)

    def add_terms(target, source):
        def step(r, _):
            part = pl.ds(pl.multiple_of(r * 16, 16), 16)
            total = source[0, part, :].astype(F32)
            for i in range(1, groups):
                total = total + source[i, part, :].astype(F32)
            target[part, :] = total
            return 0

        lax.fori_loop(0, target.shape[0] // 16, step, 0)

    add_terms(first_ref, first_recv)
    add_terms(second_ref, second_recv)

    arrived(b_recv, 3)
    from_blocks(b_recv)

    def unmix(j, _):
        picked = dot(select[...], gathered(j).astype(BF16), ((1,), (0,)))
        grad_tok_ref[:, lanes(j)] = picked.astype(BF16)
        return 0

    lax.fori_loop(0, chunks, unmix, 0)
    sent(x_send, 0)
    sent(o_send, 2)
    sent(b_send, 3)
    sent(first_send, 4)
    sent(second_send, 5)


def local(tokens, routes, gates, w_in, w_out, out_grad):
    groups, experts = lax.axis_size("dp"), lax.axis_size("expert")
    rows, width = tokens.shape
    capacity = max(2, 3 * rows * routes.shape[1] // (2 * experts))
    slots = experts * capacity
    hid = w_in.shape[2]
    chunks = width // LANES
    blocks = pltpu.VMEM((experts, capacity * chunks, LANES), BF16)
    first = pltpu.VMEM((groups, width // groups, hid), BF16)
    second = pltpu.VMEM((groups, hid, width // groups), BF16)
    vmem = pl.BlockSpec(memory_space=pltpu.VMEM)
    hbm = pl.BlockSpec(memory_space=pltpu.HBM)
    mixed, grad_tokens, grad_gates, grad_first, grad_second = pl.pallas_call(
        functools.partial(kernel, groups, experts, capacity),
        out_shape=(
            jax.ShapeDtypeStruct((rows, width), BF16),
            jax.ShapeDtypeStruct((rows, width), BF16),
            jax.ShapeDtypeStruct((rows, 1), F32),
            jax.ShapeDtypeStruct((width // groups, hid), F32),
            jax.ShapeDtypeStruct((hid, width // groups), F32),
        ),
        in_specs=[hbm, hbm, hbm, hbm, vmem, vmem],
        out_specs=[vmem] * 5,
        scratch_shapes=[
            pltpu.VMEM((rows, width), BF16),
            pltpu.VMEM((rows, width), BF16),
            pltpu.VMEM((width, hid), BF16),
            pltpu.VMEM((hid, width), BF16),
            pltpu.VMEM((rows, slots), BF16),
            pltpu.VMEM((slots * chunks, LANES), F32),
            *([blocks] * 8),
            pltpu.VMEM((slots, width), BF16),
            pltpu.VMEM((slots, width), BF16),
            pltpu.VMEM((slots, hid), F32),
            pltpu.VMEM((slots, hid), BF16),
            pltpu.VMEM((slots, hid), BF16),
            first,
            first,
            second,
            second,
            pltpu.SemaphoreType.DMA((4,)),
            pltpu.SemaphoreType.DMA((6,)),
            pltpu.SemaphoreType.DMA((6,)),
            pltpu.SemaphoreType.DMA((6,)),
        ],
        compiler_params=pltpu.CompilerParams(
            collective_id=0, has_side_effects=True, vmem_limit_bytes=50 * 2**20
        ),
        cost_estimate=pl.CostEstimate(
            flops=12 * slots * width * hid,
            bytes_accessed=12 * width * hid,
            transcendentals=2 * slots * hid,
        ),
    )(tokens, out_grad, w_in[0], w_out[0], routes, gates)
    return (mixed, grad_tokens, grad_gates, grad_first[None], grad_second[None])


def solution(mesh):
    placed = (
        P(("dp", "expert"), None),
        P(("dp", "expert"), None),
        P(("dp", "expert"), None),
        P("expert", None, None),
        P("expert", None, None),
        P(("dp", "expert"), None),
    )
    return jax.shard_map(
        local,
        mesh=mesh,
        in_specs=placed,
        out_specs=(
            P(("dp", "expert"), None),
            P(("dp", "expert"), None),
            P(("dp", "expert"), None),
            P("expert", "dp", None),
            P("expert", None, "dp"),
        ),
        check_vma=False,
    )
```

```python
import functools
import math

import jax
import jax.numpy as jnp
from jax import lax
from jax.experimental import pallas as pl
from jax.experimental.pallas import tpu as pltpu
from jax.sharding import PartitionSpec as P

MESH = pl.DeviceIdType.MESH
LANES = 128
F32 = jnp.float32
BF16 = jnp.bfloat16


def dot(left, right, dims):
    return lax.dot_general(left, right, ((dims[0], dims[1]), ((), ())), preferred_element_type=F32)


def kernel(
    groups,
    experts,
    capacity,
    tok_hbm,
    grad_hbm,
    w_in_hbm,
    w_out_hbm,
    routes_ref,
    gates_ref,
    mixed_hbm,
    grad_tok_hbm,
    grad_gates_hbm,
    first_hbm,
    second_hbm,
    mixed_ref,
    grad_tok_ref,
    grad_gates_ref,
    gates_row,
    first_ref,
    second_ref,
    tok,
    cot,
    w_in,
    w_out,
    select,
    combine,
    gates,
    stage,
    x_send,
    x_recv,
    g_send,
    g_recv,
    o_send,
    o_recv,
    b_send,
    b_recv,
    xs,
    gs,
    pre,
    hidden,
    grad_pre,
    first_send,
    first_recv,
    second_send,
    second_recv,
    load_sem,
    save_sem,
    own_sem,
    send_sem,
    recv_sem,
):
    dp = lax.axis_index("dp")
    me = lax.axis_index("expert")
    z, core = me // 2, me % 2
    ring = experts // 2
    rows, width = tok.shape
    slots = experts * capacity
    chunks = width // LANES
    block = capacity * chunks
    hid = hidden.shape[1]

    saves = [
        pltpu.make_async_copy(source, target, save_sem.at[i])
        for i, (source, target) in enumerate(
            (
                (mixed_ref, mixed_hbm),
                (gates_row, grad_gates_hbm),
                (first_ref, first_hbm),
                (second_ref, second_hbm),
                (grad_tok_ref, grad_tok_hbm),
            )
        )
    ]
    loads = [
        pltpu.make_async_copy(source, target, load_sem.at[i])
        for i, (source, target) in enumerate(
            ((tok_hbm, tok), (grad_hbm, cot), (w_in_hbm, w_in), (w_out_hbm, w_out))
        )
    ]
    for load in loads:
        load.start()

    barrier = pltpu.get_barrier_semaphore()

    def greet_expert(k, _):
        pl.semaphore_signal(
            barrier, inc=1, device_id=(dp, (me + k) % experts), device_id_type=MESH
        )
        return 0

    def greet_group(k, _):
        pl.semaphore_signal(
            barrier, inc=1, device_id=((dp + k) % groups, me), device_id_type=MESH
        )
        return 0

    lax.fori_loop(1, experts, greet_expert, 0)
    lax.fori_loop(1, groups, greet_group, 0)

    def scatter(source, target, which):
        def fill(place):
            part = stage[pl.ds(pl.multiple_of(place * block, block), block), :]
            source[place] = part.astype(BF16)

        def send(place):
            fill(place)
            pltpu.make_async_remote_copy(
                src_ref=source.at[place],
                dst_ref=target.at[me],
                send_sem=send_sem.at[which],
                recv_sem=recv_sem.at[which],
                device_id=(dp, place),
                device_id_type=MESH,
            ).start()

        def step(i, _):
            far = ring // 2 - (i + 1) // 2
            sign = 1 - 2 * (i % 2)
            there = (z + sign * far + ring) % ring
            send(there * 2 + core)
            send(there * 2 + 1 - core)
            return 0

        lax.fori_loop(0, ring - 1, step, 0)
        send(z * 2 + 1 - core)
        fill(me)
        pltpu.make_async_copy(source.at[me], target.at[me], own_sem.at[which]).start()

    def arrived(target, which):
        others = target.at[pl.ds(0, target.shape[0] - 1)]
        pltpu.make_async_copy(target.at[0], target.at[0], own_sem.at[which]).wait()
        pltpu.make_async_copy(others, others, recv_sem.at[which]).wait()

    def sent(target, which):
        others = target.at[pl.ds(0, target.shape[0] - 1)]
        pltpu.make_async_copy(others, others, send_sem.at[which]).wait()

    def spread(j, value):
        stage[pl.ds(j, slots, stride=chunks), :] = value

    def gathered(j):
        return stage[pl.ds(j, slots, stride=chunks), :]

    def lanes(j):
        return pl.ds(pl.multiple_of(j * LANES, LANES), LANES)

    def from_blocks(source):
        def step(e, _):
            stage[pl.ds(pl.multiple_of(e * block, block), block), :] = source[e].astype(F32)
            return 0

        lax.fori_loop(0, experts, step, 0, unroll=4)

    def to_rows(source, target):
        from_blocks(source)

        def step(j, _):
            target[:, lanes(j)] = gathered(j).astype(BF16)
            return 0

        lax.fori_loop(0, chunks, step, 0)

    route = routes_ref[...]
    onehot = (route == lax.broadcasted_iota(jnp.int32, (experts, rows), 0)).astype(F32)
    before = (
        lax.broadcasted_iota(jnp.int32, (rows, rows), 0)
        < lax.broadcasted_iota(jnp.int32, (rows, rows), 1)
    ).astype(BF16)
    earlier = dot(onehot.astype(BF16), before, ((1,), (0,)))
    slot = jnp.sum(onehot * earlier, axis=0, keepdims=True).astype(jnp.int32)
    place = route * capacity + slot
    chosen = (place == lax.broadcasted_iota(jnp.int32, (slots, rows), 0)).astype(F32)
    select[...] = chosen.astype(BF16)

    loads[0].wait()

    def pick_tokens(j, _):
        spread(j, dot(select[...], tok[:, lanes(j)], ((1,), (0,))))
        return 0

    lax.fori_loop(0, chunks, pick_tokens, 0)
    pl.semaphore_wait(barrier, experts - 1 + groups - 1)
    scatter(x_send, x_recv, 0)

    gates[...] = jnp.transpose(jnp.broadcast_to(gates_ref[...], (rows, rows)))[:, :1]
    loads[1].wait()

    def pick_grads(j, _):
        scaled = (gates[...] * cot[:, lanes(j)].astype(F32)).astype(BF16)
        spread(j, dot(select[...], scaled, ((1,), (0,))))
        return 0

    lax.fori_loop(0, chunks, pick_grads, 0)
    scatter(g_send, g_recv, 1)

    combine[...] = jnp.transpose(chosen).astype(BF16)

    loads[2].wait()
    loads[3].wait()
    arrived(x_recv, 0)
    to_rows(x_recv, xs)

    def wide(j):
        return pl.ds(pl.multiple_of(j * 256, 256), 256)

    def forward(j, _):
        value = dot(xs[...], w_in[:, wide(j)], ((1,), (0,)))
        pre[:, wide(j)] = value
        hidden[:, wide(j)] = (value / (1.0 + jnp.exp(-value))).astype(BF16)
        return 0

    lax.fori_loop(0, hid // 256, forward, 0)

    def project(j, _):
        value = dot(hidden[...], w_out[:, wide(j)], ((1,), (0,)))
        spread(2 * j, value[:, :LANES])
        spread(2 * j + 1, value[:, LANES:])
        return 0

    lax.fori_loop(0, width // 256, project, 0)
    sent(g_send, 1)
    scatter(o_send, o_recv, 2)

    arrived(g_recv, 1)
    to_rows(g_recv, gs)

    def backward(j, _):
        value = dot(gs[...], w_out[wide(j), :], ((1,), (1,)))
        at = pre[:, wide(j)]
        sig = 1.0 / (1.0 + jnp.exp(-at))
        grad_pre[:, wide(j)] = (value * sig * (1.0 + at * (1.0 - sig))).astype(BF16)
        return 0

    lax.fori_loop(0, hid // 256, backward, 0)

    side = math.isqrt(groups)

    def weight_terms(k, _):
        turn = k * 5 % groups
        to = (dp // side + turn // side) % side * side + (dp + turn) % side
        first_send[to] = dot(xs[:, lanes(to)], grad_pre[...], ((0,), (0,))).astype(BF16)
        second_send[to] = dot(hidden[...], gs[:, lanes(to)], ((0,), (0,))).astype(BF16)
        return to

    def share(k, _):
        to = weight_terms(k, 0)
        for which, source, target in ((4, first_send, first_recv), (5, second_send, second_recv)):
            pltpu.make_async_remote_copy(
                src_ref=source.at[to],
                dst_ref=target.at[dp],
                send_sem=send_sem.at[which],
                recv_sem=recv_sem.at[which],
                device_id=(to, me),
                device_id_type=MESH,
            ).start()
        return 0

    lax.fori_loop(1, groups, share, 0)
    weight_terms(0, 0)
    for which, source, target in ((4, first_send, first_recv), (5, second_send, second_recv)):
        pltpu.make_async_copy(source.at[dp], target.at[dp], own_sem.at[which]).start()

    def unproject(j, _):
        value = dot(grad_pre[...], w_in[wide(j), :], ((1,), (1,)))
        spread(2 * j, value[:, :LANES])
        spread(2 * j + 1, value[:, LANES:])
        return 0

    lax.fori_loop(0, width // 256, unproject, 0)
    scatter(b_send, b_recv, 3)

    arrived(o_recv, 2)
    from_blocks(o_recv)
    grad_gates_ref[...] = jnp.zeros_like(grad_gates_ref)

    def mix(j, _):
        picked = dot(combine[...], gathered(j).astype(BF16), ((1,), (0,)))
        mixed_ref[:, lanes(j)] = (gates[...] * picked).astype(BF16)
        grad_gates_ref[...] += jnp.sum(
            picked * cot[:, lanes(j)].astype(F32), axis=1, keepdims=True
        )
        return 0

    lax.fori_loop(0, chunks, mix, 0)
    gates_row[...] = jnp.transpose(jnp.broadcast_to(grad_gates_ref[...], (rows, rows)))[:1, :]
    saves[0].start()
    saves[1].start()

    arrived(first_recv, 4)
    arrived(second_recv, 5)

    def add_terms(target, source):
        def step(r, _):
            part = pl.ds(pl.multiple_of(r * 16, 16), 16)
            total = source[0, part, :].astype(F32)
            for i in range(1, groups):
                total = total + source[i, part, :].astype(F32)
            target[part, :] = total
            return 0

        lax.fori_loop(0, target.shape[0] // 16, step, 0)

    add_terms(first_ref, first_recv)
    add_terms(second_ref, second_recv)
    saves[2].start()
    saves[3].start()

    arrived(b_recv, 3)
    from_blocks(b_recv)

    def unmix(j, _):
        picked = dot(combine[...], gathered(j).astype(BF16), ((1,), (0,)))
        grad_tok_ref[:, lanes(j)] = picked.astype(BF16)
        return 0

    lax.fori_loop(0, chunks, unmix, 0)
    saves[4].start()
    for save in saves:
        save.wait()
    sent(x_send, 0)
    sent(o_send, 2)
    sent(b_send, 3)
    sent(first_send, 4)
    sent(second_send, 5)


def hand_over(*refs):
    sources, targets, held, come, gone = refs[:5], refs[5:10], refs[10:15], refs[15], refs[16]
    loads = [pltpu.make_async_copy(sources[i], held[i], come.at[i]) for i in range(5)]
    saves = [pltpu.make_async_copy(held[i], targets[i], gone.at[i]) for i in range(5)]
    for load in loads:
        load.start()
    for load, save in zip(loads, saves):
        load.wait()
        save.start()
    for save in saves:
        save.wait()


def local(tokens, routes, gates, w_in, w_out, out_grad):
    groups, experts = lax.axis_size("dp"), lax.axis_size("expert")
    rows, width = tokens.shape
    capacity = max(2, 3 * rows * routes.shape[1] // (2 * experts))
    slots = experts * capacity
    hid = w_in.shape[2]
    chunks = width // LANES
    blocks = pltpu.VMEM((experts, capacity * chunks, LANES), BF16)
    first = pltpu.VMEM((groups, width // groups, hid), BF16)
    second = pltpu.VMEM((groups, hid, width // groups), BF16)
    vmem = pl.BlockSpec(memory_space=pltpu.VMEM)
    hbm = pl.BlockSpec(memory_space=pl.ANY)
    results = pl.pallas_call(
        functools.partial(kernel, groups, experts, capacity),
        out_shape=(
            jax.ShapeDtypeStruct((rows, width), BF16),
            jax.ShapeDtypeStruct((rows, width), BF16),
            jax.ShapeDtypeStruct((1, rows), F32),
            jax.ShapeDtypeStruct((width // groups, hid), F32),
            jax.ShapeDtypeStruct((hid, width // groups), F32),
        ),
        in_specs=[hbm, hbm, hbm, hbm, vmem, vmem],
        out_specs=[hbm] * 5,
        scratch_shapes=[
            pltpu.VMEM((rows, width), BF16),
            pltpu.VMEM((rows, width), BF16),
            pltpu.VMEM((rows, 1), F32),
            pltpu.VMEM((1, rows), F32),
            pltpu.VMEM((width // groups, hid), F32),
            pltpu.VMEM((hid, width // groups), F32),
            pltpu.VMEM((rows, width), BF16),
            pltpu.VMEM((rows, width), BF16),
            pltpu.VMEM((width, hid), BF16),
            pltpu.VMEM((hid, width), BF16),
            pltpu.VMEM((slots, rows), BF16),
            pltpu.VMEM((rows, slots), BF16),
            pltpu.VMEM((rows, 1), F32),
            pltpu.VMEM((slots * chunks, LANES), F32),
            *([blocks] * 8),
            pltpu.VMEM((slots, width), BF16),
            pltpu.VMEM((slots, width), BF16),
            pltpu.VMEM((slots, hid), F32),
            pltpu.VMEM((slots, hid), BF16),
            pltpu.VMEM((slots, hid), BF16),
            first,
            first,
            second,
            second,
            pltpu.SemaphoreType.DMA((4,)),
            pltpu.SemaphoreType.DMA((5,)),
            pltpu.SemaphoreType.DMA((6,)),
            pltpu.SemaphoreType.DMA((6,)),
            pltpu.SemaphoreType.DMA((6,)),
        ],
        compiler_params=pltpu.CompilerParams(
            collective_id=0, has_side_effects=True, vmem_limit_bytes=62 * 2**20
        ),
        cost_estimate=pl.CostEstimate(
            flops=12 * slots * width * hid,
            bytes_accessed=12 * width * hid,
            transcendentals=2 * slots * hid,
        ),
    )(tokens, out_grad, w_in[0], w_out[0], routes.reshape(1, rows), gates.reshape(1, rows))
    mixed, grad_tokens, grad_gates, grad_first, grad_second = pl.pallas_call(
        hand_over,
        out_shape=[jax.ShapeDtypeStruct(r.shape, r.dtype) for r in results],
        in_specs=[hbm] * 5,
        out_specs=[hbm] * 5,
        scratch_shapes=[
            *(pltpu.VMEM(r.shape, r.dtype) for r in results),
            pltpu.SemaphoreType.DMA((5,)),
            pltpu.SemaphoreType.DMA((5,)),
        ],
        compiler_params=pltpu.CompilerParams(vmem_limit_bytes=62 * 2**20),
    )(*results)
    return (
        mixed,
        grad_tokens,
        grad_gates.reshape(rows, 1),
        grad_first[None],
        grad_second[None],
    )


def solution(mesh):
    placed = (
        P(("dp", "expert"), None),
        P(("dp", "expert"), None),
        P(("dp", "expert"), None),
        P("expert", None, None),
        P("expert", None, None),
        P(("dp", "expert"), None),
    )
    return jax.shard_map(
        local,
        mesh=mesh,
        in_specs=placed,
        out_specs=(
            P(("dp", "expert"), None),
            P(("dp", "expert"), None),
            P(("dp", "expert"), None),
            P("expert", "dp", None),
            P("expert", None, "dp"),
        ),
        check_vma=False,
    )
```

```python
import functools
import math

import jax
import jax.numpy as jnp
from jax import lax
from jax.experimental import pallas as pl
from jax.experimental.pallas import tpu as pltpu
from jax.sharding import PartitionSpec as P

MESH = pl.DeviceIdType.MESH
LANES = 128
F32 = jnp.float32
BF16 = jnp.bfloat16


def dot(left, right, dims):
    return lax.dot_general(left, right, ((dims[0], dims[1]), ((), ())), preferred_element_type=F32)


def kernel(
    groups,
    experts,
    capacity,
    tok_hbm,
    grad_hbm,
    w_in_hbm,
    w_out_hbm,
    routes_ref,
    gates_ref,
    mixed_hbm,
    grad_tok_hbm,
    grad_gates_hbm,
    first_hbm,
    second_hbm,
    mixed_ref,
    grad_tok_ref,
    grad_gates_ref,
    gates_row,
    first_ref,
    second_ref,
    tok,
    cot,
    w_in,
    w_out,
    select,
    combine,
    gates,
    stage,
    x_send,
    x_recv,
    g_send,
    g_recv,
    o_send,
    o_recv,
    b_send,
    b_recv,
    xs,
    gs,
    pre,
    hidden,
    grad_pre,
    first_send,
    first_recv,
    second_send,
    second_recv,
    load_sem,
    save_sem,
    own_sem,
    send_sem,
    recv_sem,
):
    dp = lax.axis_index("dp")
    me = lax.axis_index("expert")
    z, core = me // 2, me % 2
    ring = experts // 2
    rows, width = tok.shape
    slots = experts * capacity
    chunks = width // LANES
    block = capacity * chunks
    hid = hidden.shape[1]

    saves = [
        pltpu.make_async_copy(source, target, save_sem.at[i])
        for i, (source, target) in enumerate(
            (
                (mixed_ref, mixed_hbm),
                (gates_row, grad_gates_hbm),
                (first_ref, first_hbm),
                (second_ref, second_hbm),
                (grad_tok_ref, grad_tok_hbm),
            )
        )
    ]
    loads = [
        pltpu.make_async_copy(source, target, load_sem.at[i])
        for i, (source, target) in enumerate(
            ((tok_hbm, tok), (grad_hbm, cot), (w_in_hbm, w_in), (w_out_hbm, w_out))
        )
    ]
    for load in loads:
        load.start()

    barrier = pltpu.get_barrier_semaphore()

    def greet_expert(k, _):
        pl.semaphore_signal(
            barrier, inc=1, device_id=(dp, (me + k) % experts), device_id_type=MESH
        )
        return 0

    def greet_group(k, _):
        pl.semaphore_signal(
            barrier, inc=1, device_id=((dp + k) % groups, me), device_id_type=MESH
        )
        return 0

    lax.fori_loop(1, experts, greet_expert, 0)
    lax.fori_loop(1, groups, greet_group, 0)

    def scatter(source, target, which):
        def fill(place):
            part = stage[pl.ds(pl.multiple_of(place * block, block), block), :]
            source[place] = part.astype(BF16)

        def send(place):
            fill(place)
            pltpu.make_async_remote_copy(
                src_ref=source.at[place],
                dst_ref=target.at[me],
                send_sem=send_sem.at[which],
                recv_sem=recv_sem.at[which],
                device_id=(dp, place),
                device_id_type=MESH,
            ).start()

        def step(i, _):
            far = i // 2 + 1 if which == 0 else ring // 2 - (i + 1) // 2
            sign = 1 - 2 * (i % 2)
            there = (z + sign * far + ring) % ring
            send(there * 2 + core)
            send(there * 2 + 1 - core)
            return 0

        lax.fori_loop(0, ring - 1, step, 0)
        send(z * 2 + 1 - core)
        fill(me)
        pltpu.make_async_copy(source.at[me], target.at[me], own_sem.at[which]).start()

    def arrived(target, which):
        others = target.at[pl.ds(0, target.shape[0] - 1)]
        pltpu.make_async_copy(target.at[0], target.at[0], own_sem.at[which]).wait()
        pltpu.make_async_copy(others, others, recv_sem.at[which]).wait()

    def sent(target, which):
        others = target.at[pl.ds(0, target.shape[0] - 1)]
        pltpu.make_async_copy(others, others, send_sem.at[which]).wait()

    def spread(j, value):
        stage[pl.ds(j, slots, stride=chunks), :] = value

    def gathered(j):
        return stage[pl.ds(j, slots, stride=chunks), :]

    def lanes(j):
        return pl.ds(pl.multiple_of(j * LANES, LANES), LANES)

    def from_blocks(source):
        def step(e, _):
            stage[pl.ds(pl.multiple_of(e * block, block), block), :] = source[e].astype(F32)
            return 0

        lax.fori_loop(0, experts, step, 0, unroll=4)

    def to_rows(source, target):
        from_blocks(source)

        def step(j, _):
            target[:, lanes(j)] = gathered(j).astype(BF16)
            return 0

        lax.fori_loop(0, chunks, step, 0)

    route = routes_ref[...]
    onehot = (route == lax.broadcasted_iota(jnp.int32, (experts, rows), 0)).astype(F32)
    before = (
        lax.broadcasted_iota(jnp.int32, (rows, rows), 0)
        < lax.broadcasted_iota(jnp.int32, (rows, rows), 1)
    ).astype(BF16)
    earlier = dot(onehot.astype(BF16), before, ((1,), (0,)))
    slot = jnp.sum(onehot * earlier, axis=0, keepdims=True).astype(jnp.int32)
    place = route * capacity + slot
    chosen = (place == lax.broadcasted_iota(jnp.int32, (slots, rows), 0)).astype(F32)
    select[...] = chosen.astype(BF16)

    loads[0].wait()

    def pick_tokens(j, _):
        spread(j, dot(select[...], tok[:, lanes(j)], ((1,), (0,))))
        return 0

    lax.fori_loop(0, chunks, pick_tokens, 0)
    pl.semaphore_wait(barrier, experts - 1 + groups - 1)
    scatter(x_send, x_recv, 0)

    gates[...] = jnp.transpose(jnp.broadcast_to(gates_ref[...], (rows, rows)))[:, :1]
    loads[1].wait()

    def pick_grads(j, _):
        scaled = (gates[...] * cot[:, lanes(j)].astype(F32)).astype(BF16)
        spread(j, dot(select[...], scaled, ((1,), (0,))))
        return 0

    lax.fori_loop(0, chunks, pick_grads, 0)
    scatter(g_send, g_recv, 1)

    combine[...] = jnp.transpose(chosen).astype(BF16)

    loads[2].wait()
    loads[3].wait()
    arrived(x_recv, 0)
    to_rows(x_recv, xs)

    def wide(j):
        return pl.ds(pl.multiple_of(j * 256, 256), 256)

    def forward(j, _):
        value = dot(xs[...], w_in[:, wide(j)], ((1,), (0,)))
        pre[:, wide(j)] = value
        hidden[:, wide(j)] = (value / (1.0 + jnp.exp(-value))).astype(BF16)
        return 0

    lax.fori_loop(0, hid // 256, forward, 0)

    def project(j, _):
        value = dot(hidden[...], w_out[:, wide(j)], ((1,), (0,)))
        spread(2 * j, value[:, :LANES])
        spread(2 * j + 1, value[:, LANES:])
        return 0

    lax.fori_loop(0, width // 256, project, 0)
    sent(g_send, 1)
    scatter(o_send, o_recv, 2)

    arrived(g_recv, 1)
    to_rows(g_recv, gs)

    def backward(j, _):
        value = dot(gs[...], w_out[wide(j), :], ((1,), (1,)))
        at = pre[:, wide(j)]
        sig = 1.0 / (1.0 + jnp.exp(-at))
        grad_pre[:, wide(j)] = (value * sig * (1.0 + at * (1.0 - sig))).astype(BF16)
        return 0

    lax.fori_loop(0, hid // 256, backward, 0)

    side = math.isqrt(groups)

    def weight_terms(k, _):
        turn = k * 5 % groups
        to = (dp // side + turn // side) % side * side + (dp + turn) % side
        first_send[to] = dot(xs[:, lanes(to)], grad_pre[...], ((0,), (0,))).astype(BF16)
        second_send[to] = dot(hidden[...], gs[:, lanes(to)], ((0,), (0,))).astype(BF16)
        return to

    def share(k, _):
        to = weight_terms(k, 0)
        for which, source, target in ((4, first_send, first_recv), (5, second_send, second_recv)):
            pltpu.make_async_remote_copy(
                src_ref=source.at[to],
                dst_ref=target.at[dp],
                send_sem=send_sem.at[which],
                recv_sem=recv_sem.at[which],
                device_id=(to, me),
                device_id_type=MESH,
            ).start()
        return 0

    lax.fori_loop(1, groups, share, 0)
    weight_terms(0, 0)
    for which, source, target in ((4, first_send, first_recv), (5, second_send, second_recv)):
        pltpu.make_async_copy(source.at[dp], target.at[dp], own_sem.at[which]).start()

    def unproject(j, _):
        value = dot(grad_pre[...], w_in[wide(j), :], ((1,), (1,)))
        spread(2 * j, value[:, :LANES])
        spread(2 * j + 1, value[:, LANES:])
        return 0

    lax.fori_loop(0, width // 256, unproject, 0)
    scatter(b_send, b_recv, 3)

    arrived(o_recv, 2)
    from_blocks(o_recv)
    grad_gates_ref[...] = jnp.zeros_like(grad_gates_ref)

    def mix(j, _):
        picked = dot(combine[...], gathered(j).astype(BF16), ((1,), (0,)))
        mixed_ref[:, lanes(j)] = (gates[...] * picked).astype(BF16)
        grad_gates_ref[...] += jnp.sum(
            picked * cot[:, lanes(j)].astype(F32), axis=1, keepdims=True
        )
        return 0

    lax.fori_loop(0, chunks, mix, 0)
    gates_row[...] = jnp.transpose(jnp.broadcast_to(grad_gates_ref[...], (rows, rows)))[:1, :]
    saves[0].start()
    saves[1].start()

    arrived(first_recv, 4)
    arrived(second_recv, 5)

    def add_terms(target, source):
        def step(r, _):
            part = pl.ds(pl.multiple_of(r * 16, 16), 16)
            total = source[0, part, :].astype(F32)
            for i in range(1, groups):
                total = total + source[i, part, :].astype(F32)
            target[part, :] = total
            return 0

        lax.fori_loop(0, target.shape[0] // 16, step, 0)

    add_terms(first_ref, first_recv)
    add_terms(second_ref, second_recv)
    saves[2].start()
    saves[3].start()

    arrived(b_recv, 3)
    from_blocks(b_recv)

    def unmix(j, _):
        picked = dot(combine[...], gathered(j).astype(BF16), ((1,), (0,)))
        grad_tok_ref[:, lanes(j)] = picked.astype(BF16)
        return 0

    lax.fori_loop(0, chunks, unmix, 0)
    saves[4].start()
    for save in saves:
        save.wait()
    sent(x_send, 0)
    sent(o_send, 2)
    sent(b_send, 3)
    sent(first_send, 4)
    sent(second_send, 5)


def hand_over(*refs):
    sources, targets, held, come, gone = refs[:5], refs[5:10], refs[10:15], refs[15], refs[16]
    loads = [pltpu.make_async_copy(sources[i], held[i], come.at[i]) for i in range(5)]
    saves = [pltpu.make_async_copy(held[i], targets[i], gone.at[i]) for i in range(5)]
    for load in loads:
        load.start()
    for load, save in zip(loads, saves):
        load.wait()
        save.start()
    for save in saves:
        save.wait()


def local(tokens, routes, gates, w_in, w_out, out_grad):
    groups, experts = lax.axis_size("dp"), lax.axis_size("expert")
    rows, width = tokens.shape
    capacity = max(2, 3 * rows * routes.shape[1] // (2 * experts))
    slots = experts * capacity
    hid = w_in.shape[2]
    chunks = width // LANES
    blocks = pltpu.VMEM((experts, capacity * chunks, LANES), BF16)
    first = pltpu.VMEM((groups, width // groups, hid), BF16)
    second = pltpu.VMEM((groups, hid, width // groups), BF16)
    vmem = pl.BlockSpec(memory_space=pltpu.VMEM)
    hbm = pl.BlockSpec(memory_space=pl.ANY)
    results = pl.pallas_call(
        functools.partial(kernel, groups, experts, capacity),
        out_shape=(
            jax.ShapeDtypeStruct((rows, width), BF16),
            jax.ShapeDtypeStruct((rows, width), BF16),
            jax.ShapeDtypeStruct((1, rows), F32),
            jax.ShapeDtypeStruct((width // groups, hid), F32),
            jax.ShapeDtypeStruct((hid, width // groups), F32),
        ),
        in_specs=[hbm, hbm, hbm, hbm, vmem, vmem],
        out_specs=[hbm] * 5,
        scratch_shapes=[
            pltpu.VMEM((rows, width), BF16),
            pltpu.VMEM((rows, width), BF16),
            pltpu.VMEM((rows, 1), F32),
            pltpu.VMEM((1, rows), F32),
            pltpu.VMEM((width // groups, hid), F32),
            pltpu.VMEM((hid, width // groups), F32),
            pltpu.VMEM((rows, width), BF16),
            pltpu.VMEM((rows, width), BF16),
            pltpu.VMEM((width, hid), BF16),
            pltpu.VMEM((hid, width), BF16),
            pltpu.VMEM((slots, rows), BF16),
            pltpu.VMEM((rows, slots), BF16),
            pltpu.VMEM((rows, 1), F32),
            pltpu.VMEM((slots * chunks, LANES), F32),
            *([blocks] * 8),
            pltpu.VMEM((slots, width), BF16),
            pltpu.VMEM((slots, width), BF16),
            pltpu.VMEM((slots, hid), F32),
            pltpu.VMEM((slots, hid), BF16),
            pltpu.VMEM((slots, hid), BF16),
            first,
            first,
            second,
            second,
            pltpu.SemaphoreType.DMA((4,)),
            pltpu.SemaphoreType.DMA((5,)),
            pltpu.SemaphoreType.DMA((6,)),
            pltpu.SemaphoreType.DMA((6,)),
            pltpu.SemaphoreType.DMA((6,)),
        ],
        compiler_params=pltpu.CompilerParams(
            collective_id=0, has_side_effects=True, vmem_limit_bytes=62 * 2**20
        ),
        cost_estimate=pl.CostEstimate(
            flops=12 * slots * width * hid,
            bytes_accessed=12 * width * hid,
            transcendentals=2 * slots * hid,
        ),
    )(tokens, out_grad, w_in[0], w_out[0], routes.reshape(1, rows), gates.reshape(1, rows))
    mixed, grad_tokens, grad_gates, grad_first, grad_second = pl.pallas_call(
        hand_over,
        out_shape=[jax.ShapeDtypeStruct(r.shape, r.dtype) for r in results],
        in_specs=[hbm] * 5,
        out_specs=[hbm] * 5,
        scratch_shapes=[
            *(pltpu.VMEM(r.shape, r.dtype) for r in results),
            pltpu.SemaphoreType.DMA((5,)),
            pltpu.SemaphoreType.DMA((5,)),
        ],
        compiler_params=pltpu.CompilerParams(vmem_limit_bytes=62 * 2**20),
    )(*results)
    return (
        mixed,
        grad_tokens,
        grad_gates.reshape(rows, 1),
        grad_first[None],
        grad_second[None],
    )


def solution(mesh):
    placed = (
        P(("dp", "expert"), None),
        P(("dp", "expert"), None),
        P(("dp", "expert"), None),
        P("expert", None, None),
        P("expert", None, None),
        P(("dp", "expert"), None),
    )
    return jax.shard_map(
        local,
        mesh=mesh,
        in_specs=placed,
        out_specs=(
            P(("dp", "expert"), None),
            P(("dp", "expert"), None),
            P(("dp", "expert"), None),
            P("expert", "dp", None),
            P("expert", None, "dp"),
        ),
        check_vma=False,
    )
```
